512 devices in a mesh: seq: 64 (over x, z_lo, core), head: 8 (over y, z_hi).
Axes of the slice: x: 4, y: 4, z: 16 (z_hi: 2, z_lo: 8; z = z_hi * 8 + z_lo), core: 2. Of those that a mesh axis runs over, the one named last changes fastest.
Arguments:
- queries: bfloat16 [16384, 8192], P(('seq', 'head')), may hold values from -8 to 8
- cache_keys: bfloat16 [4096, 1024], P('seq', 'head'), may hold values from -4 to 4
- cache_values: bfloat16 [4096, 1024], P('seq', 'head'), may hold values from -4 to 4
- slab_keys: bfloat16 [16384, 1024], P('seq', 'head'), may hold values from -4 to 4
- slab_values: bfloat16 [16384, 1024], P('seq', 'head'), may hold values from -4 to 4
- block_lists: int32 [64, 256, 24], P('head', 'seq'), may hold values from 0 to 63, as said below
Outputs:
- attended: bfloat16 [16384, 8192], P(('seq', 'head'))
The draws below stay inside these ranges and needn't reach their ends.
Inputs may be any that keep to these rules, and one draw needn't show every extreme that they name: `block_lists`: for each head and query block the 24 entries are distinct. Entries 0 to 11 are the head's vertical blocks, the same for all its query blocks, all below 32, the first one 0. Entry 12 + j of query block q is 32 + (o_j + q) mod (32) for the head's own distinct offsets o_j.
All inputs are finite; a program needn't handle non-finite values.
Results may differ from the reference program's by a relative error of at most 0.0049.
Values may be sent and summed in bfloat16 or wider, within the bound.
No kernel may reach another device: no remote copies, remote signals or barrier semaphores. Data moves between devices by JAX's collectives and lax.ppermute only.
A program may use at most 64 MiB of HBM per device.

```python
import jax
import jax.numpy as jnp
from jax import lax

HEADS = 64
KVH = 8
DH = 128
BLOCK = 64
NV = 12
NS = 12
WIN = 4
SLAB = 16384
CACHE = 4096
QB = 256
CB = 64
GROUP = 8
LIST = 24


def draw_slab_keys(key, part):
    key = jax.random.fold_in(key, 11)
    return jnp.clip(jax.random.normal(key, (SLAB, KVH * DH), jnp.float32), -4.0, 4.0).astype(jnp.bfloat16)


def draw_queries(key, part):
    key = jax.random.fold_in(key, 12)
    return jnp.clip(jax.random.normal(key, (SLAB, HEADS * DH), jnp.float32), -4.0, 4.0).astype(jnp.bfloat16)


def draw_block_lists(key, part):
    key = jax.random.fold_in(key, 13)
    half = CB // 2
    column_key, slash_key = jax.random.split(key)

    def vertical_one(subkey):
        shuffled = jax.random.permutation(subkey, half - 1) + 1
        return jnp.concatenate([jnp.zeros((1,), jnp.int32), shuffled[:NV - 1].astype(jnp.int32)])

    def slash_one(subkey):
        return jax.random.permutation(subkey, half)[:NS].astype(jnp.int32)
    columns = jax.vmap(vertical_one)(jax.random.split(column_key, HEADS))
    slash_offsets = jax.vmap(slash_one)(jax.random.split(slash_key, HEADS))
    positions = jnp.arange(QB, dtype=jnp.int32)
    slashes = half + (slash_offsets[:, None, :] + positions[None, :, None]) % half
    verticals = jnp.broadcast_to(columns[:, None, :], (HEADS, QB, NV))
    return jnp.concatenate([verticals, slashes], axis=2).astype(jnp.int32)


def shard_levels(key, shape, cuts, least, top_value):
    level, own = 1.0, jax.random.fold_in(key, 6)
    for axis_at, blocks in cuts:
        steps = jnp.exp(jax.random.uniform(jax.random.fold_in(own, axis_at), (blocks,), jnp.float32, least / len(cuts), top_value / len(cuts)))
        level = level * jnp.repeat(steps, shape[axis_at] // blocks).reshape([-1 if axis == axis_at else 1 for axis in range(len(shape))])
    return level


def scatter_about(rng, dims, width, bound, pieces=(), kind=jnp.bfloat16):
    result = width * jax.random.normal(rng, dims, jnp.float32)
    if pieces:
        result = result * shard_levels(rng, dims, pieces, -0.22, 0.18)
    return jnp.clip(result, -bound, bound).astype(kind)


def setup_inputs(seed: int = 0) -> dict:
    key_list = jax.random.split(jax.random.key(seed), 7)
    queries = draw_queries(jax.random.fold_in(key_list[6], 71), 0)
    cache_keys = scatter_about(key_list[1], (CACHE, KVH * DH), 1.0, 4.0, ((0, 64), (1, 8)))
    cache_values = scatter_about(key_list[2], (CACHE, KVH * DH), 1.0, 4.0, ((0, 64), (1, 8)))
    slab_keys = draw_slab_keys(jax.random.fold_in(key_list[6], 71), 0)
    slab_values = scatter_about(key_list[4], (SLAB, KVH * DH), 1.0, 4.0, ((0, 64), (1, 8)))
    block_lists = draw_block_lists(jax.random.fold_in(key_list[6], 71), 0)
    return dict(queries=queries, cache_keys=cache_keys, cache_values=cache_values, slab_keys=slab_keys, slab_values=slab_values, block_lists=block_lists)


def softmax_weights(logit_matrix, allowed):
    masked = jnp.where(allowed, logit_matrix, -jnp.inf)
    highest = jnp.max(masked, axis=-1, keepdims=True)
    raised = jnp.exp(masked - highest)
    return (raised / jnp.sum(raised, axis=-1, keepdims=True)).astype(jnp.bfloat16)


def reference(queries, cache_keys, cache_values, slab_keys, slab_values, block_lists):
    query_blocks = jnp.arange(QB, dtype=jnp.int32)
    offsets = jnp.arange(WIN, dtype=jnp.int32)
    slab_position = query_blocks[:, None] - offsets[None, :]
    slab_valid = slab_position >= 0
    slab_index = jnp.maximum(slab_position, 0).astype(jnp.int32)
    rows_in_block = jnp.arange(BLOCK, dtype=jnp.int32)
    causal = rows_in_block[None, :] <= rows_in_block[:, None]
    slab_mask = slab_valid[:, None, :, None] & ((offsets[None, None, :, None] > 0) | causal[None, :, None, :])
    slab_mask = slab_mask.reshape(QB, BLOCK, WIN * BLOCK)
    full_mask = jnp.concatenate([jnp.ones((QB, BLOCK, LIST * BLOCK), dtype=bool), slab_mask], axis=2)
    score_scale = DH ** -0.5

    def one_head(head_number):
        kv_number = head_number // GROUP
        query_tile_rows = lax.dynamic_slice_in_dim(queries, head_number * DH, DH, 1)
        query_tile_rows = query_tile_rows.astype(jnp.float32).reshape(QB, BLOCK, DH)
        cache_k = lax.dynamic_slice_in_dim(cache_keys, kv_number * DH, DH, 1).reshape(CB, BLOCK, DH)
        cache_v = lax.dynamic_slice_in_dim(cache_values, kv_number * DH, DH, 1).reshape(CB, BLOCK, DH)
        slab_k = lax.dynamic_slice_in_dim(slab_keys, kv_number * DH, DH, 1).reshape(QB, BLOCK, DH)
        slab_v = lax.dynamic_slice_in_dim(slab_values, kv_number * DH, DH, 1).reshape(QB, BLOCK, DH)
        lists = lax.dynamic_index_in_dim(block_lists, head_number, 0, keepdims=False).astype(jnp.int32)
        selected_key_rows = jnp.concatenate([
            jnp.take(cache_k, lists, axis=0).reshape(QB, LIST * BLOCK, DH),
            jnp.take(slab_k, slab_index, axis=0).reshape(QB, WIN * BLOCK, DH)], axis=1).astype(jnp.float32)
        selected_value_rows = jnp.concatenate([
            jnp.take(cache_v, lists, axis=0).reshape(QB, LIST * BLOCK, DH),
            jnp.take(slab_v, slab_index, axis=0).reshape(QB, WIN * BLOCK, DH)], axis=1).astype(jnp.float32)
        logit_matrix = jnp.einsum("yav,ycv->yac", query_tile_rows, selected_key_rows) * score_scale
        probability_weights = lax.optimization_barrier(softmax_weights(logit_matrix, full_mask))
        weighted_total = jnp.einsum("fgx,fxc->fgc", probability_weights.astype(jnp.float32), selected_value_rows)
        return weighted_total.astype(jnp.bfloat16)

    results = lax.map(one_head, jnp.arange(HEADS, dtype=jnp.int32))
    return results.reshape(HEADS, SLAB, DH).transpose(1, 0, 2).reshape(SLAB, HEADS * DH)
```

```python
import functools
import math

import jax
import jax.numpy as jnp
from jax import lax
from jax.experimental import pallas as pl
from jax.experimental.pallas import tpu as pltpu
from jax.sharding import PartitionSpec as P

DH = 128
BLOCK = 64
NV = 12
WIN = 4
X, ZL, CORE = 4, 8, 2
CHUNKS = 2
NEG = -1e30
HEADS_A_STEP = 4


def attention_kernel(
    lists_ref, spot_ref, near_ref, far_ref, halo_ref, own_ref, *rest, pieces, blocks, listed
):
    piece_refs, (near_out, far_out, cache_ref, sem) = rest[:pieces], rest[pieces:]
    head = pl.program_id(0)
    rows = piece_refs[0].shape[0]
    half = BLOCK // 2

    @pl.when(head == 0)
    def _():
        copies = [
            pltpu.make_async_copy(ref, cache_ref.at[pl.ds(rows * i, rows)], sem.at[i])
            for i, ref in enumerate(piece_refs)
        ]
        for copy in copies:
            copy.start()
        for copy in copies:
            copy.wait()

    for lane in range(HEADS_A_STEP):
        base = (head * HEADS_A_STEP + lane) * (blocks * listed)
        lanes = slice(lane * DH, (lane + 1) * DH)
        factor = DH**-0.5 * math.log2(math.e)

        def rows_of(entry):
            return pl.ds(pl.multiple_of(lists_ref[entry] * BLOCK, BLOCK), BLOCK)

        def pick(entries, column):
            return jnp.concatenate(
                [cache_ref[rows_of(e), pl.ds(column, DH)] for e in entries], axis=0
            )

        def scores(a, b):
            return lax.dot_general(a, b, (((1,), (1,)), ((), ())), preferred_element_type=jnp.float32)

        def mix(a, b):
            return lax.dot_general(a, b, (((1,), (0,)), ((), ())), preferred_element_type=jnp.float32)

        def both(entries_0, entries_1, b, column):
            return jnp.concatenate(
                [
                    jnp.concatenate([pick(entries_0, column), window(b, column)], axis=0),
                    jnp.concatenate([pick(entries_1, column), window(b + 1, column)], axis=0),
                ],
                axis=1,
            )

        def window(b, column):
            parts = []
            if b < WIN - 1:
                parts.append(halo_ref[b * BLOCK : (WIN - 1) * BLOCK, column : column + DH])
            parts.append(own_ref[0 : (b + 1) * BLOCK, column : column + DH])
            return jnp.concatenate(parts, axis=0)

        vertical = [base + j for j in range(NV)]
        q = jnp.concatenate(
            [ref[half * b : half * (b + 1), lanes] for b in range(blocks) for ref in (near_ref, far_ref)], axis=0
        )
        s_vertical = scores(q, pick(vertical, 0))
        window_at = (listed - NV) * BLOCK
        column = lax.broadcasted_iota(jnp.int32, (2 * BLOCK, WIN * BLOCK), 1)
        row = lax.broadcasted_iota(jnp.int32, (2 * BLOCK, WIN * BLOCK), 0)
        second = row >= BLOCK
        row = row % BLOCK
        row = jnp.where(row < half, row + spot_ref[1] * half, row - spot_ref[1] * half)
        causal = column <= row + (WIN - 1) * BLOCK
        first = spot_ref[0] == 0
        blank = jnp.zeros((BLOCK, DH), jnp.bfloat16)

        weights, mixes, totals = [], [], []
        for b in range(0, blocks, 2):
            here = slice(b * BLOCK, (b + 2) * BLOCK)
            slash = [[base + c * listed + j for j in range(NV, listed)] for c in (b, b + 1)]
            q_pair = jnp.concatenate(
                [
                    jnp.concatenate([q[b * BLOCK : (b + 1) * BLOCK], blank], axis=1),
                    jnp.concatenate([blank, q[(b + 1) * BLOCK : (b + 2) * BLOCK]], axis=1),
                ],
                axis=0,
            )
            s_v = s_vertical[here]
            s_p = scores(q_pair, both(*slash, b, 0))
            s_s, s_w = s_p[:, :window_at], s_p[:, window_at:]
            lowest = jnp.where(second, WIN - 2 - b, WIN - 1 - b) * jnp.where(first, BLOCK, 0)
            s_w = jnp.where(causal & (column >= lowest), s_w, NEG)
            top = jnp.maximum(
                jnp.maximum(jnp.max(s_v, axis=1, keepdims=True), jnp.max(s_s, axis=1, keepdims=True)),
                jnp.max(s_w, axis=1, keepdims=True),
            )
            shift = top * factor
            p_v = jnp.exp2(s_v * factor - shift)
            p_s = jnp.exp2(s_s * factor - shift)
            p_w = jnp.exp2(s_w * factor - shift)
            totals.append(
                jnp.sum(p_v, axis=1, keepdims=True)
                + jnp.sum(p_s, axis=1, keepdims=True)
                + jnp.sum(p_w, axis=1, keepdims=True)
            )
            weights.append(p_v.astype(jnp.bfloat16))
            p_p = jnp.concatenate([p_s.astype(jnp.bfloat16), p_w.astype(jnp.bfloat16)], axis=1)
            mixed = mix(p_p, both(*slash, b, DH))
            mixes += [mixed[:BLOCK, :DH], mixed[BLOCK:, DH:]]
        mixed = mix(jnp.concatenate(weights, axis=0), pick(vertical, DH)) + jnp.concatenate(mixes, axis=0)
        mixed = (mixed / jnp.concatenate(totals, axis=0)).astype(jnp.bfloat16)
        for b in range(blocks):
            near_out[half * b : half * (b + 1), lanes] = mixed[BLOCK * b : BLOCK * b + half]
            far_out[half * b : half * (b + 1), lanes] = mixed[BLOCK * b + half : BLOCK * (b + 1)]


def attention(lists, spot, near, far, halo, own, pieces, start, heads):
    group, blocks, listed = lists.shape
    tokens = far.shape[0]
    whole = pl.BlockSpec(memory_space=pltpu.VMEM)
    part = jax.ShapeDtypeStruct((tokens, heads * DH), jnp.bfloat16)
    return pl.pallas_call(
        functools.partial(attention_kernel, pieces=len(pieces), blocks=blocks, listed=listed),
        grid_spec=pltpu.PrefetchScalarGridSpec(
            num_scalar_prefetch=2,
            grid=(heads // HEADS_A_STEP,),
            in_specs=[
                pl.BlockSpec((tokens, HEADS_A_STEP * DH), lambda h, _, spot: (0, (spot[1] * group + start) // HEADS_A_STEP + h)),
                pl.BlockSpec((tokens, HEADS_A_STEP * DH), lambda h, *_: (0, h)),
                whole,
                whole,
                *[pl.BlockSpec(memory_space=pl.ANY)] * len(pieces),
            ],
            out_specs=[pl.BlockSpec((tokens, HEADS_A_STEP * DH), lambda h, *_: (0, h))] * 2,
            scratch_shapes=[
                pltpu.VMEM((sum(p.shape[0] for p in pieces), 2 * DH), jnp.bfloat16),
                pltpu.SemaphoreType.DMA((len(pieces),)),
            ],
        ),
        out_shape=[part, part],
        compiler_params=pltpu.CompilerParams(vmem_limit_bytes=40 * 2**20),
        cost_estimate=pl.CostEstimate(
            flops=8 * tokens * heads * DH * BLOCK * (listed + WIN),
            bytes_accessed=4 * 2**20,
            transcendentals=2 * tokens * heads * BLOCK * (listed + WIN),
        ),
        name="attention",
    )(lists[start : start + heads].reshape(-1), spot, near, far, halo, own, *pieces)


def per_device(queries, cache_keys, cache_values, slab_keys, slab_values, block_lists):
    count = X * ZL * CORE
    group = block_lists.shape[0]
    seq, side = lax.axis_index(("x", "zc")), lax.axis_index("zh")
    heads = group // CHUNKS

    def send(array, target):
        return lax.ppermute(array, ("x", "zc"), [(i, target(i)) for i in range(count)])

    def over_side(array):
        return lax.ppermute(array, "zh", [(0, 1), (1, 0)])

    slab = jnp.concatenate([slab_keys, slab_values], axis=1)
    halo = lax.ppermute(
        slab[-(WIN - 1) * BLOCK :], ("x", "zc"), [(i, i + 1) for i in range(count - 1)]
    )

    held = jnp.concatenate([cache_keys, cache_values], axis=1)
    order = [0]
    for bit in (4, 2, 1):
        held = jnp.concatenate([held, send(held, lambda i: i ^ (bit * CORE))], axis=0)
        order += [p | bit for p in order]
        if bit == 4:
            queries, held = lax.optimization_barrier((queries, held))
            near = lax.all_to_all(queries, "y", split_axis=1, concat_axis=0, tiled=True)
    leaving = [
        lax.dynamic_slice_in_dim(
            near, ((1 - side) * group + chunk * heads) * DH, heads * DH, axis=1
        )
        for chunk in range(CHUNKS)
    ]
    leaving, held, halo = lax.optimization_barrier((leaving, held, halo))
    far = [over_side(part) for part in leaving]
    copies = jnp.broadcast_to(held[None], (X, *held.shape))
    along_x = lax.all_to_all(copies, "x", split_axis=0, concat_axis=0, tiled=True)
    along_x = along_x.reshape(-1, 2 * DH)
    far[0], along_x = lax.optimization_barrier((far[0], along_x))
    pieces = [along_x, send(along_x, lambda i: i ^ 1)]

    place = [order.index(p) for p in range(ZL)]
    block_x, block_z, block_core = block_lists // (ZL * CORE), block_lists // CORE % ZL, block_lists % CORE
    own_z, own_core = seq // CORE % ZL, seq % CORE
    z_bits = block_z ^ own_z
    z_place = sum(jnp.where((z_bits & bit) != 0, place[bit], 0) for bit in (4, 2, 1))
    lists = (block_core ^ own_core) * (X * ZL) + block_x * ZL + z_place

    spot = jnp.stack([seq, side])
    mine, back = [], []
    for chunk in range(CHUNKS):
        here, theirs = attention(lists, spot, near, far[chunk], halo, slab, pieces, chunk * heads, heads)
        mine.append(here)
        back.append(over_side(theirs))
    both = jnp.where(
        side == 0, jnp.concatenate(mine + back, axis=1), jnp.concatenate(back + mine, axis=1)
    )
    return lax.all_to_all(both, "y", split_axis=0, concat_axis=1, tiled=True)


def solution(mesh):
    fine = jax.sharding.Mesh(mesh.devices.reshape(X, ZL * CORE, -1, 2), ("x", "zc", "y", "zh"))
    seq, head = ("x", "zc"), ("y", "zh")
    rows, columns = P((*seq, *head), None), P(seq, head)
    return jax.shard_map(
        per_device,
        mesh=fine,
        in_specs=(rows, columns, columns, columns, columns, P(head, seq, None)),
        out_specs=rows,
        check_vma=False,
    )
```

```python
import functools
import math

import jax
import jax.numpy as jnp
from jax import lax
from jax.experimental import pallas as pl
from jax.experimental.pallas import tpu as pltpu
from jax.sharding import PartitionSpec as P

DH = 128
BLOCK = 64
NV = 12
WIN = 4
X, ZL, CORE = 4, 8, 2
NEG = -1e30
HEADS_A_STEP = 4


def attention_kernel(
    lists_ref, spot_ref, near_ref, far_ref, halo_ref, own_ref, *rest, pieces, blocks, listed
):
    piece_refs, (near_out, far_out, cache_ref, sem) = rest[:pieces], rest[pieces:]
    head = pl.program_id(0)
    rows = piece_refs[0].shape[0]
    half = BLOCK // 2

    @pl.when(head == 0)
    def _():
        copies = [
            pltpu.make_async_copy(ref, cache_ref.at[pl.ds(rows * i, rows)], sem.at[i])
            for i, ref in enumerate(piece_refs)
        ]
        for copy in copies:
            copy.start()
        for copy in copies:
            copy.wait()

    for lane in range(HEADS_A_STEP):
        base = (head * HEADS_A_STEP + lane) * (blocks * listed)
        lanes = slice(lane * DH, (lane + 1) * DH)
        factor = DH**-0.5 * math.log2(math.e)

        def rows_of(entry):
            return pl.ds(pl.multiple_of(lists_ref[entry] * BLOCK, BLOCK), BLOCK)

        def pick(entries, column):
            return jnp.concatenate(
                [cache_ref[rows_of(e), pl.ds(column, DH)] for e in entries], axis=0
            )

        def scores(a, b):
            return lax.dot_general(a, b, (((1,), (1,)), ((), ())), preferred_element_type=jnp.float32)

        def mix(a, b):
            return lax.dot_general(a, b, (((1,), (0,)), ((), ())), preferred_element_type=jnp.float32)

        def both(entries_0, entries_1, b, column):
            return jnp.concatenate(
                [
                    jnp.concatenate([pick(entries_0, column), window(b, column)], axis=0),
                    jnp.concatenate([pick(entries_1, column), window(b + 1, column)], axis=0),
                ],
                axis=1,
            )

        def window(b, column):
            parts = []
            if b < WIN - 1:
                parts.append(halo_ref[b * BLOCK : (WIN - 1) * BLOCK, column : column + DH])
            parts.append(own_ref[0 : (b + 1) * BLOCK, column : column + DH])
            return jnp.concatenate(parts, axis=0)

        vertical = [base + j for j in range(NV)]
        q = jnp.concatenate(
            [ref[half * b : half * (b + 1), lanes] for b in range(blocks) for ref in (near_ref, far_ref)], axis=0
        )
        s_vertical = scores(q, pick(vertical, 0))
        window_at = (listed - NV) * BLOCK
        column = lax.broadcasted_iota(jnp.int32, (2 * BLOCK, WIN * BLOCK), 1)
        row = lax.broadcasted_iota(jnp.int32, (2 * BLOCK, WIN * BLOCK), 0)
        second = row >= BLOCK
        row = row % BLOCK
        row = jnp.where(row < half, row + spot_ref[1] * half, row - spot_ref[1] * half)
        causal = column <= row + (WIN - 1) * BLOCK
        first = spot_ref[0] == 0
        blank = jnp.zeros((BLOCK, DH), jnp.bfloat16)

        weights, mixes, totals = [], [], []
        for b in range(0, blocks, 2):
            here = slice(b * BLOCK, (b + 2) * BLOCK)
            slash = [[base + c * listed + j for j in range(NV, listed)] for c in (b, b + 1)]
            q_pair = jnp.concatenate(
                [
                    jnp.concatenate([q[b * BLOCK : (b + 1) * BLOCK], blank], axis=1),
                    jnp.concatenate([blank, q[(b + 1) * BLOCK : (b + 2) * BLOCK]], axis=1),
                ],
                axis=0,
            )
            s_v = s_vertical[here]
            s_p = scores(q_pair, both(*slash, b, 0))
            s_s, s_w = s_p[:, :window_at], s_p[:, window_at:]
            lowest = jnp.where(second, WIN - 2 - b, WIN - 1 - b) * jnp.where(first, BLOCK, 0)
            s_w = jnp.where(causal & (column >= lowest), s_w, NEG)
            top = jnp.maximum(
                jnp.maximum(jnp.max(s_v, axis=1, keepdims=True), jnp.max(s_s, axis=1, keepdims=True)),
                jnp.max(s_w, axis=1, keepdims=True),
            )
            shift = top * factor
            p_v = jnp.exp2(s_v * factor - shift)
            p_s = jnp.exp2(s_s * factor - shift)
            p_w = jnp.exp2(s_w * factor - shift)
            totals.append(
                jnp.sum(p_v, axis=1, keepdims=True)
                + jnp.sum(p_s, axis=1, keepdims=True)
                + jnp.sum(p_w, axis=1, keepdims=True)
            )
            weights.append(p_v.astype(jnp.bfloat16))
            p_p = jnp.concatenate([p_s.astype(jnp.bfloat16), p_w.astype(jnp.bfloat16)], axis=1)
            mixed = mix(p_p, both(*slash, b, DH))
            mixes += [mixed[:BLOCK, :DH], mixed[BLOCK:, DH:]]
        mixed = mix(jnp.concatenate(weights, axis=0), pick(vertical, DH)) + jnp.concatenate(mixes, axis=0)
        mixed = (mixed / jnp.concatenate(totals, axis=0)).astype(jnp.bfloat16)
        for b in range(blocks):
            near_out[half * b : half * (b + 1), lanes] = mixed[BLOCK * b : BLOCK * b + half]
            far_out[half * b : half * (b + 1), lanes] = mixed[BLOCK * b + half : BLOCK * (b + 1)]


def attention(lists, spot, near, far, halo, own, pieces, start, heads):
    group, blocks, listed = lists.shape
    tokens = far.shape[0]
    whole = pl.BlockSpec(memory_space=pltpu.VMEM)
    part = jax.ShapeDtypeStruct((tokens, heads * DH), jnp.bfloat16)
    return pl.pallas_call(
        functools.partial(attention_kernel, pieces=len(pieces), blocks=blocks, listed=listed),
        grid_spec=pltpu.PrefetchScalarGridSpec(
            num_scalar_prefetch=2,
            grid=(heads // HEADS_A_STEP,),
            in_specs=[
                pl.BlockSpec((tokens, HEADS_A_STEP * DH), lambda h, _, spot: (0, (spot[1] * group + start) // HEADS_A_STEP + h)),
                pl.BlockSpec((tokens, HEADS_A_STEP * DH), lambda h, *_: (0, start // HEADS_A_STEP + h)),
                whole,
                whole,
                *[pl.BlockSpec(memory_space=pl.ANY)] * len(pieces),
            ],
            out_specs=[pl.BlockSpec((tokens, HEADS_A_STEP * DH), lambda h, *_: (0, h))] * 2,
            scratch_shapes=[
                pltpu.VMEM((sum(p.shape[0] for p in pieces), 2 * DH), jnp.bfloat16),
                pltpu.SemaphoreType.DMA((len(pieces),)),
            ],
        ),
        out_shape=[part, part],
        compiler_params=pltpu.CompilerParams(vmem_limit_bytes=40 * 2**20),
        cost_estimate=pl.CostEstimate(
            flops=8 * tokens * heads * DH * BLOCK * (listed + WIN),
            bytes_accessed=4 * 2**20,
            transcendentals=2 * tokens * heads * BLOCK * (listed + WIN),
        ),
        name="attention",
    )(lists[start : start + heads].reshape(-1), spot, near, far, halo, own, *pieces)


def per_device(queries, cache_keys, cache_values, slab_keys, slab_values, block_lists):
    count = X * ZL * CORE
    group = block_lists.shape[0]
    seq, side = lax.axis_index(("x", "zc")), lax.axis_index("zh")

    def send(array, target):
        return lax.ppermute(array, ("x", "zc"), [(i, target(i)) for i in range(count)])

    def over_side(array):
        return lax.ppermute(array, "zh", [(0, 1), (1, 0)])

    slab = jnp.concatenate([slab_keys, slab_values], axis=1)
    tail = slab[-(WIN - 1) * BLOCK :]

    held = jnp.concatenate([cache_keys, cache_values], axis=1)
    order = [0]
    for bit in (4, 2, 1):
        held = jnp.concatenate([held, send(held, lambda i: i ^ (bit * CORE))], axis=0)
        order += [p | bit for p in order]
        if bit == 4:
            queries, held = lax.optimization_barrier((queries, held))
            near = lax.all_to_all(queries, "y", split_axis=1, concat_axis=0, tiled=True)
    leaving = lax.dynamic_slice_in_dim(near, (1 - side) * group * DH, group * DH, axis=1)
    leaving, held, tail = lax.optimization_barrier((leaving, held, tail))
    halo = lax.ppermute(tail, ("x", "zc"), [(i, i + 1) for i in range(count - 1)])
    far = over_side(leaving)
    copies = jnp.broadcast_to(held[None], (X, *held.shape))
    along_x = lax.all_to_all(copies, "x", split_axis=0, concat_axis=0, tiled=True)
    along_x = along_x.reshape(-1, 2 * DH)
    far, halo, along_x = lax.optimization_barrier((far, halo, along_x))
    pieces = [along_x, send(along_x, lambda i: i ^ 1)]

    place = [order.index(p) for p in range(ZL)]
    block_x, block_z, block_core = block_lists // (ZL * CORE), block_lists // CORE % ZL, block_lists % CORE
    own_z, own_core = seq // CORE % ZL, seq % CORE
    z_bits = block_z ^ own_z
    z_place = sum(jnp.where((z_bits & bit) != 0, place[bit], 0) for bit in (4, 2, 1))
    lists = (block_core ^ own_core) * (X * ZL) + block_x * ZL + z_place

    spot = jnp.stack([seq, side])
    mine, theirs = attention(lists, spot, near, far, halo, slab, pieces, 0, group)
    rows = queries.shape[0]
    halves = [half.reshape(-1, 1, rows, group * DH) for half in (mine, theirs)]
    both = jnp.where(side == 0, jnp.concatenate(halves, axis=1), jnp.concatenate(halves[::-1], axis=1))
    both = both.reshape(-1, group * DH)
    return lax.all_to_all(both, ("y", "zh"), split_axis=0, concat_axis=1, tiled=True)


def solution(mesh):
    fine = jax.sharding.Mesh(mesh.devices.reshape(X, ZL * CORE, -1, 2), ("x", "zc", "y", "zh"))
    seq, head = ("x", "zc"), ("y", "zh")
    rows, columns = P((*seq, *head), None), P(seq, head)
    return jax.shard_map(
        per_device,
        mesh=fine,
        in_specs=(rows, columns, columns, columns, columns, P(head, seq, None)),
        out_specs=rows,
        check_vma=False,
    )
```

```python
import functools
import math

import jax
import jax.numpy as jnp
from jax import lax
from jax.experimental import pallas as pl
from jax.experimental.pallas import tpu as pltpu
from jax.sharding import PartitionSpec as P

DH = 128
BLOCK = 64
NV = 12
WIN = 4
X, ZL, CORE = 4, 8, 2
NEG = -1e30
HEADS_A_STEP = 4


def attention_kernel(
    lists_ref, spot_ref, near_ref, far_ref, halo_ref, own_ref, *rest, pieces, blocks, listed
):
    piece_refs, (near_out, far_out, cache_ref, sem) = rest[:pieces], rest[pieces:]
    head = pl.program_id(0)
    rows = piece_refs[0].shape[0]
    half = BLOCK // 2

    @pl.when(head == 0)
    def _():
        copies = [
            pltpu.make_async_copy(ref, cache_ref.at[pl.ds(rows * i, rows)], sem.at[i])
            for i, ref in enumerate(piece_refs)
        ]
        for copy in copies:
            copy.start()
        for copy in copies:
            copy.wait()

    for lane in range(HEADS_A_STEP):
        base = (head * HEADS_A_STEP + lane) * (blocks * listed)
        lanes = slice(lane * DH, (lane + 1) * DH)
        factor = DH**-0.5 * math.log2(math.e)

        def rows_of(entry):
            return pl.ds(pl.multiple_of(lists_ref[entry] * BLOCK, BLOCK), BLOCK)

        def pick(entries, column):
            return jnp.concatenate(
                [cache_ref[rows_of(e), pl.ds(column, DH)] for e in entries], axis=0
            )

        def scores(a, b):
            return lax.dot_general(a, b, (((1,), (1,)), ((), ())), preferred_element_type=jnp.float32)

        def mix(a, b):
            return lax.dot_general(a, b, (((1,), (0,)), ((), ())), preferred_element_type=jnp.float32)

        def both(entries_0, entries_1, b, column):
            return jnp.concatenate(
                [
                    jnp.concatenate([pick(entries_0, column), window(b, column)], axis=0),
                    jnp.concatenate([pick(entries_1, column), window(b + 1, column)], axis=0),
                ],
                axis=1,
            )

        def window(b, column):
            parts = []
            if b < WIN - 1:
                parts.append(halo_ref[b * BLOCK : (WIN - 1) * BLOCK, column : column + DH])
            parts.append(own_ref[0 : (b + 1) * BLOCK, column : column + DH])
            return jnp.concatenate(parts, axis=0)

        vertical = [base + j for j in range(NV)]
        q = jnp.concatenate(
            [ref[half * b : half * (b + 1), lanes] for b in range(blocks) for ref in (near_ref, far_ref)], axis=0
        )
        s_vertical = scores(q, pick(vertical, 0))
        window_at = (listed - NV) * BLOCK
        column = lax.broadcasted_iota(jnp.int32, (2 * BLOCK, WIN * BLOCK), 1)
        row = lax.broadcasted_iota(jnp.int32, (2 * BLOCK, WIN * BLOCK), 0)
        second = row >= BLOCK
        row = row % BLOCK
        row = jnp.where(row < half, row + spot_ref[1] * half, row - spot_ref[1] * half)
        causal = column <= row + (WIN - 1) * BLOCK
        first = spot_ref[0] == 0
        blank = jnp.zeros((BLOCK, DH), jnp.bfloat16)

        weights, mixes, totals = [], [], []
        for b in range(0, blocks, 2):
            here = slice(b * BLOCK, (b + 2) * BLOCK)
            slash = [[base + c * listed + j for j in range(NV, listed)] for c in (b, b + 1)]
            q_pair = jnp.concatenate(
                [
                    jnp.concatenate([q[b * BLOCK : (b + 1) * BLOCK], blank], axis=1),
                    jnp.concatenate([blank, q[(b + 1) * BLOCK : (b + 2) * BLOCK]], axis=1),
                ],
                axis=0,
            )
            s_v = s_vertical[here]
            s_p = scores(q_pair, both(*slash, b, 0))
            s_s, s_w = s_p[:, :window_at], s_p[:, window_at:]
            lowest = jnp.where(second, WIN - 2 - b, WIN - 1 - b) * jnp.where(first, BLOCK, 0)
            s_w = jnp.where(causal & (column >= lowest), s_w, NEG)
            top = jnp.maximum(
                jnp.maximum(jnp.max(s_v, axis=1, keepdims=True), jnp.max(s_s, axis=1, keepdims=True)),
                jnp.max(s_w, axis=1, keepdims=True),
            )
            shift = top * factor
            p_v = jnp.exp2(s_v * factor - shift)
            p_s = jnp.exp2(s_s * factor - shift)
            p_w = jnp.exp2(s_w * factor - shift)
            totals.append(
                jnp.sum(p_v, axis=1, keepdims=True)
                + jnp.sum(p_s, axis=1, keepdims=True)
                + jnp.sum(p_w, axis=1, keepdims=True)
            )
            weights.append(p_v.astype(jnp.bfloat16))
            p_p = jnp.concatenate([p_s.astype(jnp.bfloat16), p_w.astype(jnp.bfloat16)], axis=1)
            mixed = mix(p_p, both(*slash, b, DH))
            mixes += [mixed[:BLOCK, :DH], mixed[BLOCK:, DH:]]
        mixed = mix(jnp.concatenate(weights, axis=0), pick(vertical, DH)) + jnp.concatenate(mixes, axis=0)
        mixed = (mixed / jnp.concatenate(totals, axis=0)).astype(jnp.bfloat16)
        for b in range(blocks):
            near_out[half * b : half * (b + 1), lanes] = mixed[BLOCK * b : BLOCK * b + half]
            far_out[half * b : half * (b + 1), lanes] = mixed[BLOCK * b + half : BLOCK * (b + 1)]


def attention(lists, spot, near, far, halo, own, pieces, start, heads):
    group, blocks, listed = lists.shape
    tokens = far.shape[0]
    whole = pl.BlockSpec(memory_space=pltpu.VMEM)
    part = jax.ShapeDtypeStruct((tokens, heads * DH), jnp.bfloat16)
    return pl.pallas_call(
        functools.partial(attention_kernel, pieces=len(pieces), blocks=blocks, listed=listed),
        grid_spec=pltpu.PrefetchScalarGridSpec(
            num_scalar_prefetch=2,
            grid=(heads // HEADS_A_STEP,),
            in_specs=[
                pl.BlockSpec((tokens, HEADS_A_STEP * DH), lambda h, _, spot: (0, (spot[1] * group + start) // HEADS_A_STEP + h)),
                pl.BlockSpec((tokens, HEADS_A_STEP * DH), lambda h, *_: (0, start // HEADS_A_STEP + h)),
                whole,
                whole,
                *[pl.BlockSpec(memory_space=pl.ANY)] * len(pieces),
            ],
            out_specs=[pl.BlockSpec((tokens, HEADS_A_STEP * DH), lambda h, *_: (0, h))] * 2,
            scratch_shapes=[
                pltpu.VMEM((sum(p.shape[0] for p in pieces), 2 * DH), jnp.bfloat16),
                pltpu.SemaphoreType.DMA((len(pieces),)),
            ],
        ),
        out_shape=[part, part],
        compiler_params=pltpu.CompilerParams(vmem_limit_bytes=40 * 2**20),
        cost_estimate=pl.CostEstimate(
            flops=8 * tokens * heads * DH * BLOCK * (listed + WIN),
            bytes_accessed=4 * 2**20,
            transcendentals=2 * tokens * heads * BLOCK * (listed + WIN),
        ),
        name="attention",
    )(lists[start : start + heads].reshape(-1), spot, near, far, halo, own, *pieces)


def per_device(queries, cache_keys, cache_values, slab_keys, slab_values, block_lists):
    count = X * ZL * CORE
    group = block_lists.shape[0]
    seq, side = lax.axis_index(("x", "zc")), lax.axis_index("zh")

    def send(array, target):
        return lax.ppermute(array, ("x", "zc"), [(i, target(i)) for i in range(count)])

    def over_side(array):
        return lax.ppermute(array, "zh", [(0, 1), (1, 0)])

    slab = jnp.concatenate([slab_keys, slab_values], axis=1)
    tail = slab[-(WIN - 1) * BLOCK :]

    held = jnp.concatenate([cache_keys, cache_values], axis=1)
    order = [0]
    for bit in (4, 2, 1):
        held = jnp.concatenate([held, send(held, lambda i: i ^ (bit * CORE))], axis=0)
        order += [p | bit for p in order]
        if bit == 4:
            queries, held = lax.optimization_barrier((queries, held))
            near = lax.all_to_all(queries, "y", split_axis=1, concat_axis=0, tiled=True)
    leaving = lax.dynamic_slice_in_dim(near, (1 - side) * group * DH, group * DH, axis=1)
    leaving, held, tail = lax.optimization_barrier((leaving, held, tail))
    far = over_side(leaving)
    halo = lax.ppermute(tail, ("x", "zc"), [(i, i + 1) for i in range(count - 1)])
    shifted = [send(held, lambda i: (i + k * ZL * CORE) % count) for k in range(1, X)]
    far, halo, shifted = lax.optimization_barrier((far, halo, shifted))
    along_x = [held, *shifted]
    pieces = along_x + [send(piece, lambda i: i ^ 1) for piece in along_x]

    place = [order.index(p) for p in range(ZL)]
    block_x, block_z, block_core = block_lists // (ZL * CORE), block_lists // CORE % ZL, block_lists % CORE
    own_x, own_z, own_core = seq // (ZL * CORE), seq // CORE % ZL, seq % CORE
    z_bits = block_z ^ own_z
    z_place = sum(jnp.where((z_bits & bit) != 0, place[bit], 0) for bit in (4, 2, 1))
    lists = (block_core ^ own_core) * (X * ZL) + (own_x - block_x) % X * ZL + z_place

    spot = jnp.stack([seq, side])
    mine, theirs = attention(lists, spot, near, far, halo, slab, pieces, 0, group)
    rows = queries.shape[0]
    halves = [half.reshape(-1, 1, rows, group * DH) for half in (mine, theirs)]
    both = jnp.where(side == 0, jnp.concatenate(halves, axis=1), jnp.concatenate(halves[::-1], axis=1))
    both = both.reshape(-1, group * DH)
    return lax.all_to_all(both, ("y", "zh"), split_axis=0, concat_axis=1, tiled=True)


def solution(mesh):
    fine = jax.sharding.Mesh(mesh.devices.reshape(X, ZL * CORE, -1, 2), ("x", "zc", "y", "zh"))
    seq, head = ("x", "zc"), ("y", "zh")
    rows, columns = P((*seq, *head), None), P(seq, head)
    return jax.shard_map(
        per_device,
        mesh=fine,
        in_specs=(rows, columns, columns, columns, columns, P(head, seq, None)),
        out_specs=rows,
        check_vma=False,
    )
```

```python
import functools
import math

import jax
import jax.numpy as jnp
from jax import lax
from jax.experimental import pallas as pl
from jax.experimental.pallas import tpu as pltpu
from jax.sharding import PartitionSpec as P

DH = 128
BLOCK = 64
NV = 12
WIN = 4
X, ZL, CORE = 4, 8, 2
NEG = -1e30
HEADS_A_STEP = 8


def attention_kernel(
    lists_ref, spot_ref, near_ref, far_ref, halo_ref, own_ref, *rest, pieces, blocks, listed
):
    piece_refs, (near_out, far_out, cache_ref, sem) = rest[:pieces], rest[pieces:]
    head = pl.program_id(0)
    rows = piece_refs[0].shape[0]
    half = BLOCK // 2

    @pl.when(head == 0)
    def _():
        copies = [
            pltpu.make_async_copy(ref, cache_ref.at[pl.ds(rows * i, rows)], sem.at[i])
            for i, ref in enumerate(piece_refs)
        ]
        for copy in copies:
            copy.start()
        for copy in copies:
            copy.wait()

    for lane in range(HEADS_A_STEP):
        base = (head * HEADS_A_STEP + lane) * (blocks * listed)
        lanes = slice(lane * DH, (lane + 1) * DH)
        factor = DH**-0.5 * math.log2(math.e)

        def rows_of(entry):
            return pl.ds(pl.multiple_of(lists_ref[entry] * BLOCK, BLOCK), BLOCK)

        def pick(entries, column):
            return jnp.concatenate(
                [cache_ref[rows_of(e), pl.ds(column, DH)] for e in entries], axis=0
            )

        def scores(a, b):
            return lax.dot_general(a, b, (((1,), (1,)), ((), ())), preferred_element_type=jnp.float32)

        def mix(a, b):
            return lax.dot_general(a, b, (((1,), (0,)), ((), ())), preferred_element_type=jnp.float32)

        def both(entries_0, entries_1, b, column):
            return jnp.concatenate(
                [
                    jnp.concatenate([pick(entries_0, column), window(b, column)], axis=0),
                    jnp.concatenate([pick(entries_1, column), window(b + 1, column)], axis=0),
                ],
                axis=1,
            )

        def window(b, column):
            parts = []
            if b < WIN - 1:
                parts.append(halo_ref[b * BLOCK : (WIN - 1) * BLOCK, column : column + DH])
            parts.append(own_ref[0 : (b + 1) * BLOCK, column : column + DH])
            return jnp.concatenate(parts, axis=0)

        vertical = [base + j for j in range(NV)]
        q = jnp.concatenate(
            [ref[half * b : half * (b + 1), lanes] for b in range(blocks) for ref in (near_ref, far_ref)], axis=0
        )
        s_vertical = scores(q, pick(vertical, 0))
        window_at = (listed - NV) * BLOCK
        column = lax.broadcasted_iota(jnp.int32, (2 * BLOCK, WIN * BLOCK), 1)
        row = lax.broadcasted_iota(jnp.int32, (2 * BLOCK, WIN * BLOCK), 0)
        second = row >= BLOCK
        row = row % BLOCK
        row = jnp.where(row < half, row + spot_ref[1] * half, row - spot_ref[1] * half)
        causal = column <= row + (WIN - 1) * BLOCK
        first = spot_ref[0] == 0
        blank = jnp.zeros((BLOCK, DH), jnp.bfloat16)

        weights, mixes, totals = [], [], []
        for b in range(0, blocks, 2):
            here = slice(b * BLOCK, (b + 2) * BLOCK)
            slash = [[base + c * listed + j for j in range(NV, listed)] for c in (b, b + 1)]
            q_pair = jnp.concatenate(
                [
                    jnp.concatenate([q[b * BLOCK : (b + 1) * BLOCK], blank], axis=1),
                    jnp.concatenate([blank, q[(b + 1) * BLOCK : (b + 2) * BLOCK]], axis=1),
                ],
                axis=0,
            )
            s_v = s_vertical[here]
            s_p = scores(q_pair, both(*slash, b, 0))
            s_s, s_w = s_p[:, :window_at], s_p[:, window_at:]
            lowest = jnp.where(second, WIN - 2 - b, WIN - 1 - b) * jnp.where(first, BLOCK, 0)
            s_w = jnp.where(causal & (column >= lowest), s_w, NEG)
            top = jnp.maximum(
                jnp.maximum(jnp.max(s_v, axis=1, keepdims=True), jnp.max(s_s, axis=1, keepdims=True)),
                jnp.max(s_w, axis=1, keepdims=True),
            )
            shift = top * factor
            p_v = jnp.exp2(s_v * factor - shift)
            p_s = jnp.exp2(s_s * factor - shift)
            p_w = jnp.exp2(s_w * factor - shift)
            totals.append(
                jnp.sum(p_v, axis=1, keepdims=True)
                + jnp.sum(p_s, axis=1, keepdims=True)
                + jnp.sum(p_w, axis=1, keepdims=True)
            )
            weights.append(p_v.astype(jnp.bfloat16))
            p_p = jnp.concatenate([p_s.astype(jnp.bfloat16), p_w.astype(jnp.bfloat16)], axis=1)
            mixed = mix(p_p, both(*slash, b, DH))
            mixes += [mixed[:BLOCK, :DH], mixed[BLOCK:, DH:]]
        mixed = mix(jnp.concatenate(weights, axis=0), pick(vertical, DH)) + jnp.concatenate(mixes, axis=0)
        mixed = (mixed / jnp.concatenate(totals, axis=0)).astype(jnp.bfloat16)
        for b in range(blocks):
            near_out[half * b : half * (b + 1), lanes] = mixed[BLOCK * b : BLOCK * b + half]
            far_out[half * b : half * (b + 1), lanes] = mixed[BLOCK * b + half : BLOCK * (b + 1)]


def attention(lists, spot, near, far, halo, own, pieces, start, heads):
    group, blocks, listed = lists.shape
    tokens = far.shape[0]
    whole = pl.BlockSpec(memory_space=pltpu.VMEM)
    part = jax.ShapeDtypeStruct((tokens, heads * DH), jnp.bfloat16)
    return pl.pallas_call(
        functools.partial(attention_kernel, pieces=len(pieces), blocks=blocks, listed=listed),
        grid_spec=pltpu.PrefetchScalarGridSpec(
            num_scalar_prefetch=2,
            grid=(heads // HEADS_A_STEP,),
            in_specs=[
                pl.BlockSpec((tokens, HEADS_A_STEP * DH), lambda h, _, spot: (0, (spot[1] * group + start) // HEADS_A_STEP + h)),
                pl.BlockSpec((tokens, HEADS_A_STEP * DH), lambda h, *_: (0, start // HEADS_A_STEP + h)),
                whole,
                whole,
                *[pl.BlockSpec(memory_space=pl.ANY)] * len(pieces),
            ],
            out_specs=[pl.BlockSpec((tokens, HEADS_A_STEP * DH), lambda h, *_: (0, h))] * 2,
            scratch_shapes=[
                pltpu.VMEM((sum(p.shape[0] for p in pieces), 2 * DH), jnp.bfloat16),
                pltpu.SemaphoreType.DMA((len(pieces),)),
            ],
        ),
        out_shape=[part, part],
        compiler_params=pltpu.CompilerParams(vmem_limit_bytes=40 * 2**20),
        cost_estimate=pl.CostEstimate(
            flops=8 * tokens * heads * DH * BLOCK * (listed + WIN),
            bytes_accessed=4 * 2**20,
            transcendentals=2 * tokens * heads * BLOCK * (listed + WIN),
        ),
        name="attention",
    )(lists[start : start + heads].reshape(-1), spot, near, far, halo, own, *pieces)


def per_device(queries, cache_keys, cache_values, slab_keys, slab_values, block_lists):
    count = X * ZL * CORE
    group = block_lists.shape[0]
    seq, side = lax.axis_index(("x", "zc")), lax.axis_index("zh")

    def send(array, target):
        return lax.ppermute(array, ("x", "zc"), [(i, target(i)) for i in range(count)])

    def over_side(array):
        return lax.ppermute(array, "zh", [(0, 1), (1, 0)])

    slab = jnp.concatenate([slab_keys, slab_values], axis=1)
    tail = slab[-(WIN - 1) * BLOCK :]

    held = jnp.concatenate([cache_keys, cache_values], axis=1)
    order = [0]
    for bit in (4, 2, 1):
        held = jnp.concatenate([held, send(held, lambda i: i ^ (bit * CORE))], axis=0)
        order += [p | bit for p in order]
        if bit == 4:
            queries, held = lax.optimization_barrier((queries, held))
            near = lax.all_to_all(queries, "y", split_axis=1, concat_axis=0, tiled=True)
    leaving = lax.dynamic_slice_in_dim(near, (1 - side) * group * DH, group * DH, axis=1)
    leaving, held, tail = lax.optimization_barrier((leaving, held, tail))
    halo = lax.ppermute(tail, ("x", "zc"), [(i, i + 1) for i in range(count - 1)])
    far = over_side(leaving)
    copies = jnp.broadcast_to(held[None], (X, *held.shape))
    along_x = lax.all_to_all(copies, "x", split_axis=0, concat_axis=0, tiled=True)
    along_x = along_x.reshape(-1, 2 * DH)
    far, halo, along_x = lax.optimization_barrier((far, halo, along_x))
    pieces = [along_x, send(along_x, lambda i: i ^ 1)]

    place = [order.index(p) for p in range(ZL)]
    block_x, block_z, block_core = block_lists // (ZL * CORE), block_lists // CORE % ZL, block_lists % CORE
    own_z, own_core = seq // CORE % ZL, seq % CORE
    z_bits = block_z ^ own_z
    z_place = sum(jnp.where((z_bits & bit) != 0, place[bit], 0) for bit in (4, 2, 1))
    lists = (block_core ^ own_core) * (X * ZL) + block_x * ZL + z_place

    spot = jnp.stack([seq, side])
    mine, theirs = attention(lists, spot, near, far, halo, slab, pieces, 0, group)
    rows = queries.shape[0]
    halves = [half.reshape(-1, 1, rows, group * DH) for half in (mine, theirs)]
    both = jnp.where(side == 0, jnp.concatenate(halves, axis=1), jnp.concatenate(halves[::-1], axis=1))
    both = both.reshape(-1, group * DH)
    return lax.all_to_all(both, ("y", "zh"), split_axis=0, concat_axis=1, tiled=True)


def solution(mesh):
    fine = jax.sharding.Mesh(mesh.devices.reshape(X, ZL * CORE, -1, 2), ("x", "zc", "y", "zh"))
    seq, head = ("x", "zc"), ("y", "zh")
    rows, columns = P((*seq, *head), None), P(seq, head)
    return jax.shard_map(
        per_device,
        mesh=fine,
        in_specs=(rows, columns, columns, columns, columns, P(head, seq, None)),
        out_specs=rows,
        check_vma=False,
    )
```
